32 devices in a mesh: group: 2 (over y), graph: 4 (over z), member: 4 (over x, core).
Axes of the slice: x: 2, y: 2, z: 4, core: 2. Of those that a mesh axis runs over, the one named last changes fastest.
Arguments:
- fine_nodes: bfloat16 [8, 1024, 512], P(('group', 'member'), 'graph'), parts along dimension 0, may hold values from -6 to 6
- coarse_nodes: bfloat16 [8, 80, 512], P(('group', 'member')), parts along dimension 0, may hold values from -6 to 6
- edge_latents: bfloat16 [8, 3072, 512], P(('group', 'member'), 'graph'), parts along dimension 0, may hold values from -6 to 6
- edge_send: int32 [3072], P('graph'), may hold values from 0 to 367, as said below
- edge_recv: int32 [3072], P('graph'), may hold values from 0 to 367, as said below
- edge_count: int32 [4], P('graph'), may hold values from 192 to 768, as said below
- send_index: int32 [4, 4, 8], P('graph'), may hold values from 0 to 255, as said below
- send_count: int32 [4, 4], P('graph'), may hold values from 0 to 8, as said below
- edge_w1: bfloat16 [2, 1536, 512], P(None, 'graph'), may hold values from -0.15625 to 0.15625
- edge_w2: bfloat16 [2, 512, 512], P(None, 'graph'), may hold values from -0.25 to 0.25
- node_w1: bfloat16 [2, 1024, 512], P(None, 'graph'), may hold values from -0.1875 to 0.1875
- node_w2: bfloat16 [2, 512, 512], P(None, 'graph'), may hold values from -0.25 to 0.25
- edge_bias: float32 [2, 512], replicated, may hold values from -3 to 3
- edge_gain: float32 [2, 512], replicated, may hold values from 0.1 to 1.9
- node_bias: float32 [2, 512], replicated, may hold values from -3 to 3
- node_gain: float32 [2, 512], replicated, may hold values from 0.1 to 1.9
Outputs:
- fine_out: bfloat16 [8, 1024, 512], P(('group', 'member'), 'graph'), parts along dimension 0
- coarse_out: bfloat16 [8, 80, 512], P(('group', 'member')), parts along dimension 0
- edge_out: bfloat16 [8, 3072, 512], P(('group', 'member'), 'graph'), parts along dimension 0
The draws below stay inside these ranges and needn't reach their ends.
There are 2 independent parts, one for each index of `group`. The reference program is written for one: setup_inputs(seed, part) draws one part's arguments, and reference() takes and returns one part's arrays. A program takes and returns all parts, laid end to end along the dimension named above; an argument that names none is the same for every part. Nothing has to cross between parts.
Inputs may be any that keep to these rules, and one draw needn't show every extreme that they name: `edge_send`: A local index below 368; it never names a slot s of the list from p at or past send_count[p, g]. `edge_recv`: as for edge_send. `edge_count`: some index of graph has all its edge slots live. `send_index`: slots at or past the count hold 0. send_count[p, p] = 0; the list from p to (p + 1) mod 4 is full.
All inputs are finite; a program needn't handle non-finite values.
Results may differ from the reference program's by a relative error of at most 0.0085.
Values may be sent and summed in bfloat16 or wider, within the bound.
A program may use at most 64 MiB of HBM per device.

```python
import jax
import jax.numpy as jnp
from jax import lax

D = 512
NODES_DEV = 256
EDGES_DEV = 768
SLOTS = 8
LAYERS = 2
MEMBERS = 4
FINE = 1024
COARSE = 80
EDGES = 3072
TABLE = 368
N_GRAPH = 4


def shared_counts(key):
    key = jax.random.fold_in(key, 101)
    raw_count = jax.random.randint(key, (N_GRAPH, N_GRAPH), 0, SLOTS + 1)
    source = lax.broadcasted_iota(jnp.int32, (N_GRAPH, N_GRAPH), 0)
    target = lax.broadcasted_iota(jnp.int32, (N_GRAPH, N_GRAPH), 1)
    raw_count = jnp.where(target == (source + 1) % N_GRAPH, SLOTS, raw_count)
    return jnp.where(target == source, 0, raw_count).astype(jnp.int32)


def pick_endpoints(key, counts):
    split_keys = jax.random.split(key, 5)
    category = jax.random.randint(split_keys[0], (EDGES,), 0, 4)
    position = jnp.arange(EDGES, dtype=jnp.int32)
    device = position // EDGES_DEV
    coarse_pick = jax.random.randint(split_keys[1], (EDGES,), 0, COARSE)
    own_node = COARSE + jax.random.randint(split_keys[2], (EDGES,), 0, NODES_DEV)
    peer_dev = jax.random.randint(split_keys[3], (EDGES,), 0, N_GRAPH)
    slot_pick = jax.random.randint(split_keys[4], (EDGES,), 0, SLOTS)
    available = counts[peer_dev, device]
    mirror = COARSE + NODES_DEV + peer_dev * SLOTS + slot_pick % jnp.maximum(available, 1)
    chosen = jnp.where(category == 0, coarse_pick, jnp.where(jnp.logical_and(category == 3, available > 0), mirror, own_node))
    chosen = jnp.where(position == 0, TABLE - 1, chosen)
    chosen = jnp.where(position == 1, 0, chosen)
    return chosen.astype(jnp.int32)


def draw_send_count(key, part):
    return shared_counts(key)


def draw_send_index(key, part):
    counts = shared_counts(key)
    key = jax.random.fold_in(key, 2)
    picked = jax.random.randint(key, (N_GRAPH, N_GRAPH, SLOTS), 0, NODES_DEV)
    source = lax.broadcasted_iota(jnp.int32, (N_GRAPH, N_GRAPH, SLOTS), 0)
    target = lax.broadcasted_iota(jnp.int32, (N_GRAPH, N_GRAPH, SLOTS), 1)
    slot_pos = lax.broadcasted_iota(jnp.int32, (N_GRAPH, N_GRAPH, SLOTS), 2)
    picked = jnp.where(slot_pos < counts[:, :, None], picked, 0)
    marked = jnp.logical_and(source == 0, target == 1)
    picked = jnp.where(jnp.logical_and(marked, slot_pos == 0), NODES_DEV - 1, picked)
    picked = jnp.where(jnp.logical_and(marked, slot_pos == 1), 0, picked)
    return picked.astype(jnp.int32)


def draw_edge_send(key, part):
    counts = shared_counts(key)
    key = jax.random.fold_in(key, 3)
    return pick_endpoints(key, counts)


def draw_edge_recv(key, part):
    counts = shared_counts(key)
    key = jax.random.fold_in(key, 4)
    return pick_endpoints(key, counts)


def draw_edge_count(key, part):
    key = jax.random.fold_in(key, 5)
    live_count = jax.random.randint(key, (N_GRAPH,), EDGES_DEV // 4, EDGES_DEV + 1)
    busiest = jax.random.randint(jax.random.fold_in(key, 6), (), 0, N_GRAPH)
    position = jnp.arange(N_GRAPH, dtype=jnp.int32)
    return jnp.where(position == busiest, EDGES_DEV, live_count).astype(jnp.int32)


def shard_levels(own_key, dims, pieces, low, top_value):
    factor_of = 1.0
    for dim, shards_of in pieces:
        draws = jax.random.uniform(jax.random.fold_in(jax.random.fold_in(own_key, 6), dim), (shards_of,), jnp.float32, low / len(pieces), top_value / len(pieces))
        factor_of = factor_of * jnp.repeat(jnp.exp(draws), dims[dim] // shards_of).reshape((-1,) + (1,) * (len(dims) - 1 - dim))
    return factor_of


def noise(rng, dims, scale, reach, cuts=(), held_as=jnp.bfloat16):
    drawn = jax.random.normal(rng, dims, jnp.float32) * scale
    if len(cuts) > 0:
        drawn = shard_levels(rng, dims, cuts, -0.22, 0.18) * drawn
    return jnp.clip(drawn, min=-reach, max=reach).astype(held_as)


def setup_inputs(seed: int = 0, part: int = 0) -> dict:
    seeds = jax.random.split(jax.random.key(seed), 17)
    own_keys = jax.random.split(jax.random.fold_in(seeds[16], part), 17)
    fine_nodes = noise(own_keys[0], (MEMBERS, FINE, D), 1.0, 6.0, ((0, 4), (1, 4)))
    coarse_nodes = noise(own_keys[1], (MEMBERS, COARSE, D), 1.0, 6.0, ((0, 4),))
    edge_latents = noise(own_keys[2], (MEMBERS, EDGES, D), 1.0, 6.0, ((0, 4), (1, 4)))
    edge_send = draw_edge_send(jax.random.fold_in(seeds[16], 71), part)
    edge_recv = draw_edge_recv(jax.random.fold_in(seeds[16], 71), part)
    edge_count = draw_edge_count(jax.random.fold_in(seeds[16], 71), part)
    send_index = draw_send_index(jax.random.fold_in(seeds[16], 71), part)
    send_count = draw_send_count(jax.random.fold_in(seeds[16], 71), part)
    edge_w1 = noise(seeds[8], (LAYERS, 3 * D, D), (3 * D) ** -0.5, 0.15625, ((1, 4),))
    edge_w2 = noise(seeds[9], (LAYERS, D, D), D ** -0.5, 0.25, ((1, 4),))
    node_w1 = noise(seeds[10], (LAYERS, 2 * D, D), (2 * D) ** -0.5, 0.1875, ((1, 4),))
    node_w2 = noise(seeds[11], (LAYERS, D, D), D ** -0.5, 0.25, ((1, 4),))
    edge_bias = noise(seeds[12], (LAYERS, D), 0.5, 3.0, (), jnp.float32)
    edge_gain = jnp.clip(1.0 + 0.18 * jax.random.normal(seeds[13], (LAYERS, D), jnp.float32), 0.1, 1.9)
    node_bias = noise(seeds[14], (LAYERS, D), 0.5, 3.0, (), jnp.float32)
    node_gain = jnp.clip(1.0 + 0.18 * jax.random.normal(seeds[15], (LAYERS, D), jnp.float32), 0.1, 1.9)
    return {"fine_nodes": fine_nodes, "coarse_nodes": coarse_nodes, "edge_latents": edge_latents, "edge_send": edge_send, "edge_recv": edge_recv, "edge_count": edge_count, "send_index": send_index, "send_count": send_count, "edge_w1": edge_w1, "edge_w2": edge_w2, "node_w1": node_w1, "node_w2": node_w2, "edge_bias": edge_bias, "edge_gain": edge_gain, "node_bias": node_bias, "node_gain": node_gain}


def layer_norm(projected, gain_row):
    average = lax.optimization_barrier(jnp.mean(projected, axis=-1, keepdims=True))
    centered = projected - average
    variance = lax.optimization_barrier(jnp.mean(centered * centered, axis=-1, keepdims=True))
    return centered * lax.rsqrt(variance + 1e-05) * gain_row

def two_layer(inputs, first_weight, bias_row, second_weight, gain_row):
    hidden = jax.nn.silu(jnp.dot(inputs, first_weight, preferred_element_type=jnp.float32) + bias_row).astype(jnp.bfloat16)
    return layer_norm(jnp.dot(hidden, second_weight, preferred_element_type=jnp.float32), gain_row)

def resolve(local_id, send_index, send_count):
    device = (jnp.arange(EDGES, dtype=jnp.int32) // EDGES_DEV).astype(jnp.int32)
    offset = local_id - COARSE - NODES_DEV
    mirror = offset >= 0
    offset = jnp.maximum(offset, 0).astype(jnp.int32)
    peer_dev = (offset // SLOTS).astype(jnp.int32)
    slot_pos = (offset % SLOTS).astype(jnp.int32)
    remote = send_index[peer_dev, device, slot_pos]
    usable = jnp.logical_or(jnp.logical_not(mirror), slot_pos < send_count[peer_dev, device])
    global_id = jnp.where(local_id < COARSE, local_id, jnp.where(mirror, COARSE + peer_dev * NODES_DEV + remote, COARSE + device * NODES_DEV + local_id - COARSE))
    return (global_id.astype(jnp.int32), usable)

def reference(fine_nodes, coarse_nodes, edge_latents, edge_send, edge_recv, edge_count, send_index, send_count, edge_w1, edge_w2, node_w1, node_w2, edge_bias, edge_gain, node_bias, node_gain):
    send_ids, send_ok = resolve(edge_send, send_index, send_count)
    recv_ids, recv_ok = resolve(edge_recv, send_index, send_count)
    device = (jnp.arange(EDGES, dtype=jnp.int32) // EDGES_DEV).astype(jnp.int32)
    live_edge = jnp.arange(EDGES, dtype=jnp.int32) % EDGES_DEV < edge_count[device]
    kept_edge = jnp.logical_and(live_edge, recv_ok)
    zero_row = jnp.zeros((), jnp.bfloat16)
    fine_list, coarse_list, edge_list = ([], [], [])
    for member in range(MEMBERS):
        node_state = jnp.concatenate([coarse_nodes[member], fine_nodes[member]], axis=0)
        edge_state = edge_latents[member]
        for layer_idx in range(LAYERS):
            senders = jnp.where(send_ok[:, None], node_state[send_ids], zero_row)
            receivers = jnp.where(recv_ok[:, None], node_state[recv_ids], zero_row)
            inputs = jnp.concatenate([edge_state, senders, receivers], axis=1)
            update = two_layer(inputs, edge_w1[layer_idx], edge_bias[layer_idx], edge_w2[layer_idx], edge_gain[layer_idx])
            edge_state = (edge_state.astype(jnp.float32) + jnp.where(live_edge[:, None], update, jnp.float32(0.0))).astype(jnp.bfloat16)
            aggregate = jax.ops.segment_sum(jnp.where(kept_edge[:, None], update, jnp.float32(0.0)), recv_ids, num_segments=COARSE + FINE)
            node_inputs = jnp.concatenate([node_state, aggregate.astype(jnp.bfloat16)], axis=1)
            node_update = two_layer(node_inputs, node_w1[layer_idx], node_bias[layer_idx], node_w2[layer_idx], node_gain[layer_idx])
            node_state = (node_state.astype(jnp.float32) + node_update).astype(jnp.bfloat16)
        coarse_list.append(node_state[:COARSE])
        fine_list.append(node_state[COARSE:])
        edge_list.append(edge_state)
    return (jnp.stack(fine_list), jnp.stack(coarse_list), jnp.stack(edge_list))
```

```python
import functools

import jax
import jax.numpy as jnp
from jax import lax
from jax.experimental import pallas as pl
from jax.experimental.pallas import tpu as pltpu
from jax.sharding import PartitionSpec as P

BLOCK = 32
BF = jnp.bfloat16
F32 = jnp.float32
MESH = pl.DeviceIdType.MESH


def layer_norm(projected, gain_row):
    average = jnp.mean(projected, axis=-1, keepdims=True)
    centered = projected - average
    variance = jnp.mean(centered * centered, axis=-1, keepdims=True)
    return centered * lax.rsqrt(variance + 1e-05) * gain_row


def project(inputs, weight):
    full_weight = lax.all_gather(weight, "graph", axis=0, tiled=True)
    return jnp.dot(inputs, full_weight, preferred_element_type=jnp.float32)


def two_layer(inputs, first_weight, bias_row, second_weight, gain_row):
    hidden = jax.nn.silu(project(inputs, first_weight) + bias_row).astype(jnp.bfloat16)
    return layer_norm(project(hidden, second_weight), gain_row)


def scatter_rows(values, indices, count):
    return jax.vmap(
        lambda member_rows: jax.ops.segment_sum(member_rows, indices, num_segments=count)
    )(values)


def node_step(states, sum_rows, first_weight, bias_row, second_weight, gain_row):
    members, row_count, latent = states.shape
    inputs = jnp.concatenate([states, sum_rows.astype(jnp.bfloat16)], axis=2).reshape(
        members * row_count, 2 * latent
    )
    change = two_layer(inputs, first_weight, bias_row, second_weight, gain_row).reshape(
        members, row_count, latent
    )
    return (states.astype(jnp.float32) + change).astype(jnp.bfloat16)


def on_device(
    fine_nodes,
    coarse_nodes,
    edge_latents,
    edge_send,
    edge_recv,
    edge_count,
    send_index,
    send_count,
    edge_w1,
    edge_w2,
    node_w1,
    node_w2,
    edge_bias,
    edge_gain,
    node_bias,
    node_gain,
):
    peer_count = lax.axis_size("graph")
    members, owned_rows, latent = fine_nodes.shape
    slot_count = send_index.shape[2]
    coarse_total = coarse_nodes.shape[1]
    edge_slots = edge_latents.shape[1]
    mirror_base = coarse_total + owned_rows
    table_rows = mirror_base + peer_count * slot_count
    live_edge = jnp.arange(edge_slots, dtype=jnp.int32) < edge_count[0]
    send_lists = send_index[0].reshape(peer_count * slot_count)
    used_out = jnp.arange(slot_count, dtype=jnp.int32)[None, :] < send_count[0][:, None]
    counts_out = send_count.reshape(1, peer_count, 1)
    zero_row = jnp.zeros((), jnp.bfloat16)
    fine_state = fine_nodes
    coarse_state = coarse_nodes
    edge_state = edge_latents
    for layer_idx in range(edge_w1.shape[0]):
        outgoing = fine_state[:, send_lists].reshape(members, peer_count, slot_count, latent)
        incoming, counts_in = (
            lax.all_to_all(outgoing, "graph", split_axis=1, concat_axis=1, tiled=True),
            lax.all_to_all(counts_out, "graph", split_axis=1, concat_axis=1, tiled=True),
        )
        used_in = (
            jnp.arange(slot_count, dtype=jnp.int32)[None, :]
            < counts_in.reshape(peer_count)[:, None]
        )
        mirrors = jnp.where(used_in[None, :, :, None], incoming, zero_row).reshape(
            members, peer_count * slot_count, latent
        )
        node_table = jnp.concatenate([coarse_state, fine_state, mirrors], axis=1)
        table_ok = jnp.concatenate(
            [jnp.ones((mirror_base,), bool), used_in.reshape(peer_count * slot_count)]
        )
        senders = node_table[:, edge_send]
        receivers = node_table[:, edge_recv]
        inputs = jnp.concatenate([edge_state, senders, receivers], axis=2).reshape(
            members * edge_slots, 3 * latent
        )
        update = two_layer(
            inputs,
            edge_w1[layer_idx],
            edge_bias[layer_idx],
            edge_w2[layer_idx],
            edge_gain[layer_idx],
        )
        update = update.reshape(members, edge_slots, latent)
        edge_state = (
            edge_state.astype(jnp.float32)
            + jnp.where(live_edge[None, :, None], update, jnp.float32(0.0))
        ).astype(jnp.bfloat16)
        kept_edge = jnp.logical_and(live_edge, table_ok[edge_recv])
        messages = jnp.where(kept_edge[None, :, None], update, jnp.float32(0.0))
        totals = scatter_rows(messages, edge_recv, table_rows)
        coarse_part = totals[:, :coarse_total]
        own_part = totals[:, coarse_total:mirror_base]
        mirror_part = totals[:, mirror_base:].reshape(members, peer_count, slot_count, latent)
        returned = lax.all_to_all(mirror_part, "graph", split_axis=1, concat_axis=1, tiled=True)
        returned = jnp.where(used_out[None, :, :, None], returned, jnp.float32(0.0))
        own_part = own_part + scatter_rows(
            returned.reshape(members, peer_count * slot_count, latent), send_lists, owned_rows
        )
        coarse_sum = lax.psum(coarse_part, "graph")
        states = jnp.concatenate([coarse_state, fine_state], axis=1)
        sum_rows = jnp.concatenate([coarse_sum, own_part], axis=1)
        updated = node_step(
            states,
            sum_rows,
            node_w1[layer_idx],
            node_bias[layer_idx],
            node_w2[layer_idx],
            node_gain[layer_idx],
        )
        coarse_state = updated[:, :coarse_total]
        fine_state = updated[:, coarse_total:]
    return (fine_state, coarse_state, edge_state)


def mm(a, b):
    return jnp.dot(a, b, preferred_element_type=F32)


def silu(v):
    half = 0.5 * v
    return half + half * jnp.tanh(half)


def kernel(
    sizes,
    idx_ref, fine_ref, coarse_ref, edge_ref,
    ew1_ref, ew2_ref, nw1_ref, nw2_ref,
    eb_ref, eg_ref, nb_ref, ng_ref,
    fine_out, coarse_out, edge_out,
    we, wn, state, outb, tab, sumb, ret, upd, gat_s, gat_r, sct,
    own_sem, a_send, a_recv, f_send, f_recv, s_send, s_recv,
    d_send, d_recv, x_send, x_recv, out_send, out_recv, ret_send, ret_recv,
):
    planes, share, coarse_total, owned, slots_edge, latent = sizes
    group = lax.axis_index("group")
    me = lax.axis_index("graph")
    member = lax.axis_index("member")
    x = member // 2
    c = member % 2
    across = (1 - x) * 2 + c
    here = (group, me, member)
    sibling = (group, me, x * 2 + 1 - c)
    first = (group + c * (1 - 2 * group), me, member + (1 - c) * (across - member))
    second = (group + (1 - c) * (1 - 2 * group), me, member + c * (across - member))
    spot = lambda dev: dev[0] * 2 + dev[2] // 2
    mine, spot_f, spot_s = spot(here), spot(first), spot(second)
    spot_d = 3 - mine
    peers = [(d, lax.rem(me + d, planes)) for d in range(1, planes)]

    def remote(src, dst, send, recv, dev):
        copy = pltpu.make_async_remote_copy(
            src_ref=src, dst_ref=dst, send_sem=send, recv_sem=recv,
            device_id=dev, device_id_type=MESH,
        )
        copy.start()

    def wait(ref, sem):
        pltpu.make_async_copy(ref, ref, sem).wait()

    barrier = pltpu.get_barrier_semaphore()
    partners = [(group, q, member) for _, q in peers] + [first, second, sibling]
    for dev in partners:
        pl.semaphore_signal(barrier, inc=1, device_id=dev, device_id_type=MESH)

    re1, re2, rn1, rn2 = (r.shape[3] for r in (ew1_ref, ew2_ref, nw1_ref, nw2_ref))
    edge_parts = [(ew1_ref, 0, re1), (ew2_ref, re1, re2)]
    node_parts = [(nw1_ref, 0, rn1), (nw2_ref, rn1, rn2)]
    groups = [(we, 0, edge_parts), (wn, 0, node_parts), (we, 1, edge_parts), (wn, 1, node_parts)]

    for k, (buf, layer, parts) in enumerate(groups):
        for src, at, rows in parts:
            pltpu.make_async_copy(
                src.at[layer], buf.at[layer, me, :, :, pl.ds(at, rows)], own_sem.at[k]
            ).start()

    def start_a(k):
        buf, layer, parts = groups[k]
        for d, q in peers:
            for src, at, rows in parts:
                remote(
                    src.at[layer, c, mine],
                    buf.at[layer, me, c, mine, pl.ds(at, rows)],
                    a_send.at[k, d - 1], a_recv.at[k, planes - d - 1],
                    (group, q, member),
                )

    def step_a(k):
        buf, layer, _ = groups[k]
        for d, q in peers:
            piece = buf.at[layer, q, c, mine]
            wait(piece, a_recv.at[k, d - 1])
            remote(piece, piece, f_send.at[k, d - 1], f_recv.at[k, d - 1], first)
            remote(piece, piece, s_send.at[k, d - 1], s_recv.at[k, d - 1], second)

    def step_c(k):
        buf, layer, _ = groups[k]
        for d, q in peers:
            piece = buf.at[layer, q, c, spot_f]
            wait(piece, f_recv.at[k, d - 1])
            remote(piece, piece, d_send.at[k, d - 1], d_recv.at[k, d - 1], second)

    def step_d(k):
        buf, layer, _ = groups[k]
        for d, q in peers:
            wait(buf.at[layer, q, c, spot_s], s_recv.at[k, d - 1])
            wait(buf.at[layer, q, c, spot_d], d_recv.at[k, d - 1])
            block = buf.at[layer, q, c]
            remote(block, block, x_send.at[k, d - 1], x_recv.at[k, d - 1], sibling)

    def step_x(k):
        buf, layer, _ = groups[k]
        for d, q in peers:
            wait(buf.at[layer, q, 1 - c], x_recv.at[k, d - 1])
        wait(buf.at[layer, me], own_sem.at[k])

    def onehot(values, axis, size):
        shape = (size, values.shape[1]) if axis == 0 else (values.shape[0], size)
        spots = lax.broadcasted_iota(jnp.int32, shape, axis).astype(F32)
        return jnp.where(values == spots, 1.0, 0.0).astype(BF)

    table_rows = planes * BLOCK + owned
    state_rows = owned + BLOCK
    idx = idx_ref[...]
    cols = jnp.transpose(idx)
    row = lax.broadcasted_iota(jnp.int32, (BLOCK, coarse_total), 0)
    col = lax.broadcasted_iota(jnp.int32, (BLOCK, coarse_total), 1)
    pick = jnp.where((row < share) & (col == me * share + row), 1.0, 0.0).astype(BF)
    state[pl.ds(0, owned)] = fine_ref[...]
    state[pl.ds(owned, BLOCK)] = mm(pick, coarse_ref[...]).astype(BF)
    sel = onehot(cols[: planes * BLOCK, 2:3], 1, state_rows)
    sel_t = onehot(idx[2:3, : planes * BLOCK], 0, state_rows)

    def make_blocks(step):
        outb[step] = mm(sel, state[...]).astype(BF).reshape(planes, BLOCK, latent)
        tab[step, me] = outb[step, me]

    def send_blocks(step):
        for d, q in peers:
            remote(
                outb.at[step, q], tab.at[step, me],
                out_send.at[step, d - 1], out_recv.at[step, planes - d - 1],
                (group, q, member),
            )

    def wait_blocks(step):
        for d, q in peers:
            wait(tab.at[step, q], out_recv.at[step, d - 1])

    make_blocks(0)
    pl.semaphore_wait(barrier, len(partners))
    send_blocks(0)
    for k in range(4):
        start_a(k)

    gat_s[...] = onehot(cols[:, 0:1], 1, table_rows)
    gat_r[...] = onehot(cols[:, 1:2], 1, table_rows)
    sct[...] = onehot(idx[1:2, :], 0, table_rows)

    def norm(y, gain):
        centered = y - jnp.mean(y, axis=-1, keepdims=True)
        variance = jnp.mean(centered * centered, axis=-1, keepdims=True)
        return centered * lax.rsqrt(variance + 1e-05) * gain

    half = slots_edge // 2

    def edge_half(layer, part):
        rows = pl.ds(part * half, half)
        table = jnp.concatenate(
            [tab[layer].reshape(planes * BLOCK, latent), state[pl.ds(0, owned)]], axis=0
        )
        prior = (edge_ref if layer == 0 else edge_out)[rows]
        sender = mm(gat_s[rows], table).astype(BF)
        receiver = mm(gat_r[rows], table).astype(BF)
        inputs = jnp.concatenate([prior, sender, receiver], axis=1)
        w1 = we[layer, :, :, :, pl.ds(0, re1)].reshape(3 * latent, latent)
        w2 = we[layer, :, :, :, pl.ds(re1, re2)].reshape(latent, latent)
        hidden = silu(mm(inputs, w1) + eb_ref[pl.ds(layer, 1)]).astype(BF)
        update = norm(mm(hidden, w2), eg_ref[pl.ds(layer, 1)])
        live = cols[part * half : (part + 1) * half, 1:2] >= 0.0
        edge_out[rows] = (prior.astype(F32) + jnp.where(live, update, 0.0)).astype(BF)
        upd[rows] = update.astype(BF)

    def send_sums(layer):
        sums = mm(sct[pl.ds(0, planes * BLOCK)], upd[...])
        sumb[layer] = sums.astype(BF).reshape(planes, BLOCK, latent)
        for d, q in peers:
            remote(
                sumb.at[layer, q], ret.at[layer, me],
                ret_send.at[layer, d - 1], ret_recv.at[layer, planes - d - 1],
                (group, q, member),
            )
        ret[layer, me] = sumb[layer, me]
        return mm(sct[pl.ds(planes * BLOCK, owned)], upd[...])

    def node(layer, own):
        for d, q in peers:
            wait(ret.at[layer, q], ret_recv.at[layer, d - 1])
        back = mm(sel_t, ret[layer].reshape(planes * BLOCK, latent))
        total = jnp.concatenate([own + back[:owned], back[owned:]], axis=0).astype(BF)
        inputs = jnp.concatenate([state[...], total], axis=1)
        w1 = wn[layer, :, :, :, pl.ds(0, rn1)].reshape(2 * latent, latent)
        w2 = wn[layer, :, :, :, pl.ds(rn1, rn2)].reshape(latent, latent)
        hidden = silu(mm(inputs, w1) + nb_ref[pl.ds(layer, 1)]).astype(BF)
        change = norm(mm(hidden, w2), ng_ref[pl.ds(layer, 1)])
        state[...] = (state[...].astype(F32) + change).astype(BF)

    step_a(0)
    step_c(0)
    step_a(1)
    step_d(0)
    step_x(0)
    wait_blocks(0)
    step_c(1)
    edge_half(0, 0)
    step_a(2)
    step_d(1)
    edge_half(0, 1)
    own = send_sums(0)
    step_c(2)
    step_a(3)
    step_x(1)
    node(0, own)
    make_blocks(1)
    send_blocks(1)
    step_d(2)
    step_c(3)
    step_x(2)
    wait_blocks(1)
    edge_half(1, 0)
    step_d(3)
    edge_half(1, 1)
    own = send_sums(1)
    step_x(3)
    node(1, own)
    make_blocks(2)
    send_blocks(2)
    fine_out[...] = state[pl.ds(0, owned)]
    row = lax.broadcasted_iota(jnp.int32, (coarse_total, planes * BLOCK), 0)
    col = lax.broadcasted_iota(jnp.int32, (coarse_total, planes * BLOCK), 1)
    place = row
    for q in range(1, planes):
        place = place + jnp.where(row >= q * share, BLOCK - share, 0)
    unpick = jnp.where(place == col, 1.0, 0.0).astype(BF)
    wait_blocks(2)
    coarse_out[...] = mm(unpick, tab[2].reshape(planes * BLOCK, latent)).astype(BF)

    for k, (buf, layer, _) in enumerate(groups):
        for d, q in peers:
            piece = buf.at[layer, q, c, mine]
            for sem in (a_send, f_send, s_send, d_send):
                wait(piece, sem.at[k, d - 1])
            wait(buf.at[layer, q, c], x_send.at[k, d - 1])
    for d, q in peers:
        for step in range(3):
            wait(outb.at[step, q], out_send.at[step, d - 1])
        for layer in range(2):
            wait(sumb.at[layer, q], ret_send.at[layer, d - 1])


def on_device_kernel(
    fine_nodes, coarse_nodes, edge_latents, edge_send, edge_recv, edge_count,
    send_index, send_count, edge_w1, edge_w2, node_w1, node_w2,
    edge_bias, edge_gain, node_bias, node_gain,
):
    planes = lax.axis_size("graph")
    _, owned, latent = fine_nodes.shape
    coarse_total = coarse_nodes.shape[1]
    slots_edge = edge_latents.shape[1]
    slots = send_index.shape[2]
    share = coarse_total // planes
    layers = edge_w1.shape[0]
    base = coarse_total + owned
    top = planes * BLOCK

    def spread(local):
        listed = local - base
        return jnp.where(
            local < coarse_total,
            local // share * BLOCK + local % share,
            jnp.where(
                local < base,
                local - coarse_total + top,
                listed // slots * BLOCK + BLOCK - slots + listed % slots,
            ),
        )

    live = jnp.arange(slots_edge, dtype=jnp.int32) < edge_count[0]
    slot = jnp.arange(slots, dtype=jnp.int32)
    listed = jnp.where(slot[None] < send_count[0][:, None], send_index[0], -1)
    lead = jnp.arange(BLOCK - slots, dtype=jnp.int32)
    lead = jnp.where(lead < share, owned + lead, -1)
    target = jnp.concatenate(
        [jnp.broadcast_to(lead[None], (planes, BLOCK - slots)), listed], axis=1
    ).reshape(top)
    idx = jnp.stack(
        [
            spread(edge_send),
            jnp.where(live, spread(edge_recv), -1),
            jnp.pad(target, (0, slots_edge - top), constant_values=-1),
        ]
    )
    idx = jnp.pad(idx, ((0, 5), (0, 0))).astype(F32)

    def cut(weight):
        return weight.reshape(layers, 2, 4, weight.shape[1] // 8, latent)

    weights = [cut(w) for w in (edge_w1, edge_w2, node_w1, node_w2)]
    edge_rows = weights[0].shape[3] + weights[1].shape[3]
    node_rows = weights[2].shape[3] + weights[3].shape[3]
    sizes = (planes, share, coarse_total, owned, slots_edge, latent)
    vmem = pl.BlockSpec(memory_space=pltpu.VMEM)
    anywhere = pl.BlockSpec(memory_space=pl.ANY)
    per_group = pltpu.SemaphoreType.DMA((2 * layers, planes - 1))
    fine, coarse, edge = pl.pallas_call(
        functools.partial(kernel, sizes),
        out_shape=(
            jax.ShapeDtypeStruct((owned, latent), BF),
            jax.ShapeDtypeStruct((coarse_total, latent), BF),
            jax.ShapeDtypeStruct((slots_edge, latent), BF),
        ),
        in_specs=[vmem] * 4 + [anywhere] * 4 + [vmem] * 4,
        out_specs=(vmem, vmem, vmem),
        scratch_shapes=[
            pltpu.VMEM((layers, planes, 2, 4, edge_rows, latent), BF),
            pltpu.VMEM((layers, planes, 2, 4, node_rows, latent), BF),
            pltpu.VMEM((owned + BLOCK, latent), BF),
            pltpu.VMEM((3, planes, BLOCK, latent), BF),
            pltpu.VMEM((3, planes, BLOCK, latent), BF),
            pltpu.VMEM((2, planes, BLOCK, latent), BF),
            pltpu.VMEM((2, planes, BLOCK, latent), BF),
            pltpu.VMEM((slots_edge, latent), BF),
            pltpu.VMEM((slots_edge, top + owned), BF),
            pltpu.VMEM((slots_edge, top + owned), BF),
            pltpu.VMEM((top + owned, slots_edge), BF),
            pltpu.SemaphoreType.DMA((2 * layers,)),
        ]
        + [per_group] * 10
        + [pltpu.SemaphoreType.DMA((3, planes - 1))] * 2
        + [pltpu.SemaphoreType.DMA((2, planes - 1))] * 2,
        compiler_params=pltpu.CompilerParams(
            collective_id=0, has_side_effects=True, vmem_limit_bytes=50 * 1024 * 1024
        ),
    )(
        idx, fine_nodes[0], coarse_nodes[0], edge_latents[0], *weights,
        edge_bias, edge_gain, node_bias, node_gain,
    )
    return fine[None], coarse[None], edge[None]


def solution(mesh):
    placed = (
        P(("group", "member"), "graph", None),
        P(("group", "member"), None, None),
        P(("group", "member"), "graph", None),
        P("graph"),
        P("graph"),
        P("graph"),
        P("graph", None, None),
        P("graph", None),
        P(None, "graph", None),
        P(None, "graph", None),
        P(None, "graph", None),
        P(None, "graph", None),
        P(),
        P(),
        P(),
        P(),
    )
    small = dict(mesh.shape) == {"group": 2, "graph": 4, "member": 4}
    body = on_device_kernel if small else on_device
    return jax.shard_map(
        body,
        mesh=mesh,
        in_specs=placed,
        out_specs=(
            P(("group", "member"), "graph", None),
            P(("group", "member"), None, None),
            P(("group", "member"), "graph", None),
        ),
        check_vma=False,
    )
```

```python
import functools

import jax
import jax.numpy as jnp
from jax import lax
from jax.experimental import pallas as pl
from jax.experimental.pallas import tpu as pltpu
from jax.sharding import PartitionSpec as P

BLOCK = 32
BF = jnp.bfloat16
F32 = jnp.float32
MESH = pl.DeviceIdType.MESH


def layer_norm(projected, gain_row):
    average = jnp.mean(projected, axis=-1, keepdims=True)
    centered = projected - average
    variance = jnp.mean(centered * centered, axis=-1, keepdims=True)
    return centered * lax.rsqrt(variance + 1e-05) * gain_row


def project(inputs, weight):
    full_weight = lax.all_gather(weight, "graph", axis=0, tiled=True)
    return jnp.dot(inputs, full_weight, preferred_element_type=jnp.float32)


def two_layer(inputs, first_weight, bias_row, second_weight, gain_row):
    hidden = jax.nn.silu(project(inputs, first_weight) + bias_row).astype(jnp.bfloat16)
    return layer_norm(project(hidden, second_weight), gain_row)


def scatter_rows(values, indices, count):
    return jax.vmap(
        lambda member_rows: jax.ops.segment_sum(member_rows, indices, num_segments=count)
    )(values)


def node_step(states, sum_rows, first_weight, bias_row, second_weight, gain_row):
    members, row_count, latent = states.shape
    inputs = jnp.concatenate([states, sum_rows.astype(jnp.bfloat16)], axis=2).reshape(
        members * row_count, 2 * latent
    )
    change = two_layer(inputs, first_weight, bias_row, second_weight, gain_row).reshape(
        members, row_count, latent
    )
    return (states.astype(jnp.float32) + change).astype(jnp.bfloat16)


def on_device(
    fine_nodes,
    coarse_nodes,
    edge_latents,
    edge_send,
    edge_recv,
    edge_count,
    send_index,
    send_count,
    edge_w1,
    edge_w2,
    node_w1,
    node_w2,
    edge_bias,
    edge_gain,
    node_bias,
    node_gain,
):
    peer_count = lax.axis_size("graph")
    members, owned_rows, latent = fine_nodes.shape
    slot_count = send_index.shape[2]
    coarse_total = coarse_nodes.shape[1]
    edge_slots = edge_latents.shape[1]
    mirror_base = coarse_total + owned_rows
    table_rows = mirror_base + peer_count * slot_count
    live_edge = jnp.arange(edge_slots, dtype=jnp.int32) < edge_count[0]
    send_lists = send_index[0].reshape(peer_count * slot_count)
    used_out = jnp.arange(slot_count, dtype=jnp.int32)[None, :] < send_count[0][:, None]
    counts_out = send_count.reshape(1, peer_count, 1)
    zero_row = jnp.zeros((), jnp.bfloat16)
    fine_state = fine_nodes
    coarse_state = coarse_nodes
    edge_state = edge_latents
    for layer_idx in range(edge_w1.shape[0]):
        outgoing = fine_state[:, send_lists].reshape(members, peer_count, slot_count, latent)
        incoming, counts_in = (
            lax.all_to_all(outgoing, "graph", split_axis=1, concat_axis=1, tiled=True),
            lax.all_to_all(counts_out, "graph", split_axis=1, concat_axis=1, tiled=True),
        )
        used_in = (
            jnp.arange(slot_count, dtype=jnp.int32)[None, :]
            < counts_in.reshape(peer_count)[:, None]
        )
        mirrors = jnp.where(used_in[None, :, :, None], incoming, zero_row).reshape(
            members, peer_count * slot_count, latent
        )
        node_table = jnp.concatenate([coarse_state, fine_state, mirrors], axis=1)
        table_ok = jnp.concatenate(
            [jnp.ones((mirror_base,), bool), used_in.reshape(peer_count * slot_count)]
        )
        senders = node_table[:, edge_send]
        receivers = node_table[:, edge_recv]
        inputs = jnp.concatenate([edge_state, senders, receivers], axis=2).reshape(
            members * edge_slots, 3 * latent
        )
        update = two_layer(
            inputs,
            edge_w1[layer_idx],
            edge_bias[layer_idx],
            edge_w2[layer_idx],
            edge_gain[layer_idx],
        )
        update = update.reshape(members, edge_slots, latent)
        edge_state = (
            edge_state.astype(jnp.float32)
            + jnp.where(live_edge[None, :, None], update, jnp.float32(0.0))
        ).astype(jnp.bfloat16)
        kept_edge = jnp.logical_and(live_edge, table_ok[edge_recv])
        messages = jnp.where(kept_edge[None, :, None], update, jnp.float32(0.0))
        totals = scatter_rows(messages, edge_recv, table_rows)
        coarse_part = totals[:, :coarse_total]
        own_part = totals[:, coarse_total:mirror_base]
        mirror_part = totals[:, mirror_base:].reshape(members, peer_count, slot_count, latent)
        returned = lax.all_to_all(mirror_part, "graph", split_axis=1, concat_axis=1, tiled=True)
        returned = jnp.where(used_out[None, :, :, None], returned, jnp.float32(0.0))
        own_part = own_part + scatter_rows(
            returned.reshape(members, peer_count * slot_count, latent), send_lists, owned_rows
        )
        coarse_sum = lax.psum(coarse_part, "graph")
        states = jnp.concatenate([coarse_state, fine_state], axis=1)
        sum_rows = jnp.concatenate([coarse_sum, own_part], axis=1)
        updated = node_step(
            states,
            sum_rows,
            node_w1[layer_idx],
            node_bias[layer_idx],
            node_w2[layer_idx],
            node_gain[layer_idx],
        )
        coarse_state = updated[:, :coarse_total]
        fine_state = updated[:, coarse_total:]
    return (fine_state, coarse_state, edge_state)


def mm(a, b):
    return jnp.dot(a, b, preferred_element_type=F32)


def silu(v):
    half = 0.5 * v
    return half + half * jnp.tanh(half)


def kernel(
    sizes,
    send_ref, recv_ref, count_ref, list_ref, used_ref,
    fine_ref, coarse_ref, edge_ref,
    ew1_ref, ew2_ref, nw1_ref, nw2_ref,
    eb_hbm, eg_hbm, nb_hbm, ng_hbm,
    fine_out, coarse_out, edge_out,
    we, wn, state, coarse_in, eb_ref, eg_ref, nb_ref, ng_ref,
    outb, tab, sumb, ret, upd, gat_s, gat_r, sct,
    in_sem, own_sem, a_send, a_recv, f_send, f_recv, s_send, s_recv,
    d_send, d_recv, x_send, x_recv, out_send, out_recv, ret_send, ret_recv,
):
    planes, share, coarse_total, owned, slots_edge, latent = sizes
    group = lax.axis_index("group")
    me = lax.axis_index("graph")
    member = lax.axis_index("member")
    x = member // 2
    c = member % 2
    across = (1 - x) * 2 + c
    here = (group, me, member)
    sibling = (group, me, x * 2 + 1 - c)
    first = (group + c * (1 - 2 * group), me, member + (1 - c) * (across - member))
    second = (group + (1 - c) * (1 - 2 * group), me, member + c * (across - member))
    corner = (1 - group, me, across)
    spot = lambda dev: dev[0] * 2 + dev[2] // 2
    mine, spot_f, spot_s = spot(here), spot(first), spot(second)
    spot_d = 3 - mine
    peers = [(d, lax.rem(me + d, planes)) for d in range(1, planes)]
    near = [me + 1 - 2 * (me % 2), 2 - me // 2, 3 - 3 * (me // 2)]

    def remote(src, dst, send, recv, dev):
        copy = pltpu.make_async_remote_copy(
            src_ref=src, dst_ref=dst, send_sem=send, recv_sem=recv,
            device_id=dev, device_id_type=MESH,
        )
        copy.start()

    def wait(ref, sem):
        pltpu.make_async_copy(ref, ref, sem).wait()

    barrier = pltpu.get_barrier_semaphore()
    partners = [(group, q, member) for _, q in peers] + [first, second, corner, sibling]
    for dev in partners:
        pl.semaphore_signal(barrier, inc=1, device_id=dev, device_id_type=MESH)

    rows_in = [
        (fine_ref.at[0], state.at[pl.ds(0, owned)]), (coarse_ref.at[0], coarse_in),
        (edge_ref.at[0], edge_out),
        (eb_hbm, eb_ref), (eg_hbm, eg_ref), (nb_hbm, nb_ref), (ng_hbm, ng_ref),
    ]
    for n, (src, dst) in enumerate(rows_in):
        pltpu.make_async_copy(src, dst, in_sem.at[n]).start()

    def wait_in(*which):
        for n in which:
            wait(rows_in[n][1], in_sem.at[n])

    re1, re2, rn1, rn2 = (r.shape[3] for r in (ew1_ref, ew2_ref, nw1_ref, nw2_ref))
    edge_parts = [(ew1_ref, 0, re1), (ew2_ref, re1, re2)]
    node_parts = [(nw1_ref, 0, rn1), (nw2_ref, rn1, rn2)]
    groups = [(we, 0, edge_parts), (wn, 0, node_parts), (we, 1, edge_parts), (wn, 1, node_parts)]

    for k, (buf, layer, parts) in enumerate(groups):
        for src, at, rows in parts:
            pltpu.make_async_copy(
                src.at[layer], buf.at[layer, me, :, :, pl.ds(at, rows)], own_sem.at[k]
            ).start()

    def start_a(k):
        buf, layer, parts = groups[k]

        for q in near:
            for src, at, rows in parts:
                remote(
                    src.at[layer, c, mine],
                    buf.at[layer, me, c, mine, pl.ds(at, rows)],
                    a_send.at[k, q], a_recv.at[k, me], (group, q, member),
                )

    def step_a(k):
        buf, layer, _ = groups[k]
        for q in near:
            piece = buf.at[layer, q, c, mine]
            wait(piece, a_recv.at[k, q])

            remote(piece, piece, f_send.at[k, q], f_recv.at[k, q], first)
            remote(piece, piece, s_send.at[k, q], s_recv.at[k, q], second)
            remote(piece, piece, d_send.at[k, q], d_recv.at[k, q], corner)

    def step_d(k):
        buf, layer, _ = groups[k]
        for q in near:
            wait(buf.at[layer, q, c, spot_f], f_recv.at[k, q])
            wait(buf.at[layer, q, c, spot_s], s_recv.at[k, q])
            wait(buf.at[layer, q, c, spot_d], d_recv.at[k, q])
            block = buf.at[layer, q, c]
            remote(block, block, x_send.at[k, q], x_recv.at[k, q], sibling)

    def step_x(k):
        buf, layer, _ = groups[k]
        for q in near:
            wait(buf.at[layer, q, 1 - c], x_recv.at[k, q])
        wait(buf.at[layer, me], own_sem.at[k])

    def onehot(values, axis, size):
        shape = (size, values.shape[1]) if axis == 0 else (values.shape[0], size)
        spots = lax.broadcasted_iota(jnp.int32, shape, axis).astype(F32)
        return jnp.where(values == spots, 1.0, 0.0).astype(BF)

    table_rows = planes * BLOCK + owned
    state_rows = owned + BLOCK
    top = planes * BLOCK
    slots = list_ref.shape[2]

    def spread(local):
        listed = local - coarse_total - owned
        low, high = local, listed + BLOCK - slots
        for q in range(1, planes):
            low = low + jnp.where(local >= q * share, BLOCK - share, 0)
            high = high + jnp.where(listed >= q * slots, BLOCK - slots, 0)
        return jnp.where(
            local < coarse_total, low,
            jnp.where(listed < 0, local - coarse_total + top, high),
        )

    lane = lax.broadcasted_iota(jnp.int32, (1, slots_edge), 1)
    target = jnp.full((1, slots_edge), -1, jnp.int32)
    for q in range(planes):
        own_lane = lane - q * BLOCK
        target = jnp.where((own_lane >= 0) & (own_lane < share), owned + own_lane, target)
        for slot in range(slots):
            node_of = jnp.where(slot < used_ref[0, q], list_ref[0, q, slot], -1)
            target = jnp.where(own_lane == BLOCK - slots + slot, node_of, target)
    receivers = jnp.where(lane < count_ref[0], spread(recv_ref[...]), -1)
    line = lax.broadcasted_iota(jnp.int32, (8, slots_edge), 0)
    idx = jnp.where(
        line == 0, spread(send_ref[...]),
        jnp.where(line == 1, receivers, jnp.where(line == 2, target, -1)),
    ).astype(F32)
    cols = jnp.transpose(idx)
    row = lax.broadcasted_iota(jnp.int32, (top, coarse_total), 0)
    col = lax.broadcasted_iota(jnp.int32, (top, coarse_total), 1)
    place = col
    for q in range(1, planes):
        place = place + jnp.where(col >= q * share, BLOCK - share, 0)
    pick = jnp.where(row == place, 1.0, 0.0).astype(BF)
    row = lax.broadcasted_iota(jnp.int32, (BLOCK, coarse_total), 0)
    col = lax.broadcasted_iota(jnp.int32, (BLOCK, coarse_total), 1)
    pick_own = jnp.where((row < share) & (col == me * share + row), 1.0, 0.0).astype(BF)
    wait_in(0, 1)
    state[pl.ds(owned, BLOCK)] = mm(pick_own, coarse_in[...]).astype(BF)
    early = BLOCK // 2
    blocks = mm(pick, coarse_in[...]).astype(BF).reshape(planes, BLOCK, latent)
    tab[0, :, pl.ds(0, early)] = blocks[:, :early]
    sel = onehot(cols[: planes * BLOCK, 2:3], 1, state_rows)
    sel_t = onehot(idx[2:3, : planes * BLOCK], 0, state_rows)

    def part_of(step):
        return pl.ds(early, BLOCK - early) if step == 0 else pl.ds(0, BLOCK)

    def make_blocks(step):
        outb[step] = mm(sel, state[...]).astype(BF).reshape(planes, BLOCK, latent)
        tab[step, me, part_of(step)] = outb[step, me, part_of(step)]

    def send_blocks(step):
        for d, q in peers:
            remote(
                outb.at[step, q, part_of(step)], tab.at[step, me, part_of(step)],
                out_send.at[step, d - 1], out_recv.at[step, planes - d - 1],
                (group, q, member),
            )

    def wait_blocks(step):
        for d, q in peers:
            wait(tab.at[step, q, part_of(step)], out_recv.at[step, d - 1])

    make_blocks(0)
    pl.semaphore_wait(barrier, len(partners))
    start_a(0)
    send_blocks(0)
    start_a(1)

    gat_s[...] = onehot(cols[:, 0:1], 1, table_rows)
    gat_r[...] = onehot(cols[:, 1:2], 1, table_rows)
    sct[...] = onehot(idx[1:2, :], 0, table_rows)
    wait_in(2, 3, 4, 5, 6)

    def norm(y, gain):
        centered = y - jnp.mean(y, axis=-1, keepdims=True)
        variance = jnp.mean(centered * centered, axis=-1, keepdims=True)
        return centered * lax.rsqrt(variance + 1e-05) * gain

    half = slots_edge // 2

    def edge_half(layer, part):
        rows = pl.ds(part * half, half)
        table = jnp.concatenate(
            [tab[layer].reshape(planes * BLOCK, latent), state[pl.ds(0, owned)]], axis=0
        )
        prior = edge_out[rows]
        sender = mm(gat_s[rows], table).astype(BF)
        receiver = mm(gat_r[rows], table).astype(BF)
        inputs = jnp.concatenate([prior, sender, receiver], axis=1)
        w1 = we[layer, :, :, :, pl.ds(0, re1)].reshape(3 * latent, latent)
        w2 = we[layer, :, :, :, pl.ds(re1, re2)].reshape(latent, latent)
        hidden = silu(mm(inputs, w1) + eb_ref[pl.ds(layer, 1)]).astype(BF)
        update = norm(mm(hidden, w2), eg_ref[pl.ds(layer, 1)])
        live = cols[part * half : (part + 1) * half, 1:2] >= 0.0
        edge_out[rows] = (prior.astype(F32) + jnp.where(live, update, 0.0)).astype(BF)
        upd[rows] = update.astype(BF)

    def send_sums(layer):
        sums = mm(sct[pl.ds(0, planes * BLOCK)], upd[...])
        sumb[layer] = sums.astype(BF).reshape(planes, BLOCK, latent)
        for d, q in peers:
            remote(
                sumb.at[layer, q], ret.at[layer, me],
                ret_send.at[layer, d - 1], ret_recv.at[layer, planes - d - 1],
                (group, q, member),
            )
        ret[layer, me] = sumb[layer, me]
        return mm(sct[pl.ds(planes * BLOCK, owned)], upd[...])

    def node(layer, own):
        for d, q in peers:
            wait(ret.at[layer, q], ret_recv.at[layer, d - 1])
        back = mm(sel_t, ret[layer].reshape(planes * BLOCK, latent))
        total = jnp.concatenate([own + back[:owned], back[owned:]], axis=0).astype(BF)
        inputs = jnp.concatenate([state[...], total], axis=1)
        w1 = wn[layer, :, :, :, pl.ds(0, rn1)].reshape(2 * latent, latent)
        w2 = wn[layer, :, :, :, pl.ds(rn1, rn2)].reshape(latent, latent)
        hidden = silu(mm(inputs, w1) + nb_ref[pl.ds(layer, 1)]).astype(BF)
        change = norm(mm(hidden, w2), ng_ref[pl.ds(layer, 1)])
        state[...] = (state[...].astype(F32) + change).astype(BF)

    step_a(0)
    step_a(1)
    step_d(0)
    start_a(2)
    step_x(0)
    wait_blocks(0)
    edge_half(0, 0)
    step_a(2)
    step_d(1)
    edge_half(0, 1)
    own = send_sums(0)
    start_a(3)
    step_x(1)
    node(0, own)
    make_blocks(1)
    send_blocks(1)
    step_a(3)
    step_d(2)
    step_x(2)
    wait_blocks(1)
    edge_half(1, 0)
    step_d(3)
    edge_half(1, 1)
    own = send_sums(1)
    step_x(3)
    node(1, own)
    make_blocks(2)
    send_blocks(2)
    fine_out[...] = state[pl.ds(0, owned)]
    row = lax.broadcasted_iota(jnp.int32, (coarse_total, top), 0)
    col = lax.broadcasted_iota(jnp.int32, (coarse_total, top), 1)
    place = row
    for q in range(1, planes):
        place = place + jnp.where(row >= q * share, BLOCK - share, 0)
    unpick = jnp.where(place == col, 1.0, 0.0).astype(BF)
    for k, (buf, layer, _) in enumerate(groups):
        for q in near:
            piece = buf.at[layer, q, c, mine]
            wait(piece, a_send.at[k, q])
            for sem in (f_send, s_send, d_send):
                wait(piece, sem.at[k, q])
            wait(buf.at[layer, q, c], x_send.at[k, q])
    for d, q in peers:
        for step in range(3):
            wait(outb.at[step, q, part_of(step)], out_send.at[step, d - 1])
        for layer in range(2):
            wait(sumb.at[layer, q], ret_send.at[layer, d - 1])
    wait_blocks(2)
    coarse_out[...] = mm(unpick, tab[2].reshape(top, latent)).astype(BF)


def on_device_kernel(
    fine_nodes, coarse_nodes, edge_latents, edge_send, edge_recv, edge_count,
    send_index, send_count, edge_w1, edge_w2, node_w1, node_w2,
    edge_bias, edge_gain, node_bias, node_gain,
):
    planes = lax.axis_size("graph")
    _, owned, latent = fine_nodes.shape
    coarse_total = coarse_nodes.shape[1]
    slots_edge = edge_latents.shape[1]
    share = coarse_total // planes
    layers = edge_w1.shape[0]
    top = planes * BLOCK

    def cut(weight):
        return weight.reshape(layers, 2, 4, weight.shape[1] // 8, latent)

    weights = [cut(w) for w in (edge_w1, edge_w2, node_w1, node_w2)]
    edge_rows = weights[0].shape[3] + weights[1].shape[3]
    node_rows = weights[2].shape[3] + weights[3].shape[3]
    sizes = (planes, share, coarse_total, owned, slots_edge, latent)
    vmem = pl.BlockSpec(memory_space=pltpu.VMEM)
    smem = pl.BlockSpec(memory_space=pltpu.SMEM)
    hbm = pl.BlockSpec(memory_space=pltpu.HBM)
    per_group = pltpu.SemaphoreType.DMA((2 * layers, planes))
    fine, coarse, edge = pl.pallas_call(
        functools.partial(kernel, sizes),
        out_shape=(
            jax.ShapeDtypeStruct((owned, latent), BF),
            jax.ShapeDtypeStruct((coarse_total, latent), BF),
            jax.ShapeDtypeStruct((slots_edge, latent), BF),
        ),
        in_specs=[vmem] * 2 + [smem] * 3 + [hbm] * 11,
        out_specs=(vmem, vmem, vmem),
        scratch_shapes=[
            pltpu.VMEM((layers, planes, 2, 4, edge_rows, latent), BF),
            pltpu.VMEM((layers, planes, 2, 4, node_rows, latent), BF),
            pltpu.VMEM((owned + BLOCK, latent), BF),
            pltpu.VMEM((coarse_total, latent), BF),
        ]
        + [pltpu.VMEM((layers, latent), F32)] * 4
        + [
            pltpu.VMEM((3, planes, BLOCK, latent), BF),
            pltpu.VMEM((3, planes, BLOCK, latent), BF),
            pltpu.VMEM((2, planes, BLOCK, latent), BF),
            pltpu.VMEM((2, planes, BLOCK, latent), BF),
            pltpu.VMEM((slots_edge, latent), BF),
            pltpu.VMEM((slots_edge, top + owned), BF),
            pltpu.VMEM((slots_edge, top + owned), BF),
            pltpu.VMEM((top + owned, slots_edge), BF),
            pltpu.SemaphoreType.DMA((7,)),
        ]
        + [pltpu.SemaphoreType.DMA((2 * layers,))]
        + [per_group] * 10
        + [pltpu.SemaphoreType.DMA((3, planes - 1))] * 2
        + [pltpu.SemaphoreType.DMA((2, planes - 1))] * 2,
        compiler_params=pltpu.CompilerParams(
            collective_id=0, has_side_effects=True, vmem_limit_bytes=62 * 1024 * 1024
        ),
    )(
        edge_send[None], edge_recv[None], edge_count, send_index, send_count,
        fine_nodes, coarse_nodes, edge_latents, *weights,
        edge_bias, edge_gain, node_bias, node_gain,
    )
    return fine[None], coarse[None], edge[None]


def solution(mesh):
    placed = (
        P(("group", "member"), "graph", None),
        P(("group", "member"), None, None),
        P(("group", "member"), "graph", None),
        P("graph"),
        P("graph"),
        P("graph"),
        P("graph", None, None),
        P("graph", None),
        P(None, "graph", None),
        P(None, "graph", None),
        P(None, "graph", None),
        P(None, "graph", None),
        P(),
        P(),
        P(),
        P(),
    )
    small = dict(mesh.shape) == {"group": 2, "graph": 4, "member": 4}
    body = on_device_kernel if small else on_device
    return jax.shard_map(
        body,
        mesh=mesh,
        in_specs=placed,
        out_specs=(
            P(("group", "member"), "graph", None),
            P(("group", "member"), None, None),
            P(("group", "member"), "graph", None),
        ),
        check_vma=False,
    )
```
